512 devices in a mesh: vr: 16 (over z_hi, y), vc: 32 (over x, z_lo, core).
Axes of the slice: x: 4, y: 4, z: 16 (z_hi: 4, z_lo: 4; z = z_hi * 4 + z_lo), core: 2. Of those that a mesh axis runs over, the one named last changes fastest.
Arguments:
- amplitudes: float32 [1024, 102400], P('vr', 'vc'), may hold values from -6 to 6
- integrals: float32 [5120, 102400], P('vr', 'vc'), may hold values from -0.01953125 to 0.01953125
- mirror_slot: int32 [1024], P('vc'), may hold values from 0 to 31, as said below
Outputs:
- residual: float32 [5120, 1024], P('vr', 'vc')
The draws below stay inside these ranges and needn't reach their ends.
Inputs may be any that keep to these rules, and one draw needn't show every extreme that they name: Occupied pairs come in 32 blocks of 32; the mirror ji of the pair in block k at position s lies in block (k + 16) mod 32 at position mirror_slot of it, and the relation is mutual: q(q(p)) = p. Within each block the slots form a permutation.
All inputs are finite; a program needn't handle non-finite values.
Results may differ from the reference program's by a relative error of at most 0.000096.
Values sent between devices are 32-bit elements; how exact they have to be, the bound alone decides.
No kernel may reach another device: no remote copies, remote signals or barrier semaphores. Data moves between devices by JAX's collectives and lax.ppermute only.
A program may use at most 64 MiB of HBM per device.

```python
import jax
import jax.numpy as jnp
from jax import lax

NIJ = 1024
CD = 102400
AB = 5120
BLOCKS = 32
ROW_BLOCK = 32
N_VC = 32


def draw_mirror_slot(key, part):
    key = jax.random.fold_in(key, 7)
    half_count = BLOCKS // 2
    subkeys = jax.random.split(key, half_count)
    forward = jax.vmap(lambda subkey: jax.random.permutation(subkey, ROW_BLOCK))(subkeys)
    backward = jnp.argsort(forward, axis=1)
    return jnp.concatenate([forward, backward], 0).reshape(-1).astype(jnp.int32)


def spiked(result, own_key, source, target, shards_of, factor):
    owner, partner = [(jnp.arange(result.shape[axis_at]) // (result.shape[axis_at] // shards_of)).reshape([-1 if axis == axis_at else 1 for axis in range(result.ndim)]) for axis_at in (source, target)]
    chosen = jax.random.permutation(own_key, shards_of)[partner]
    strong = (owner == chosen) | (owner == (partner + shards_of // 2) % shards_of)
    return jnp.where(strong, factor * result, result)


def steps_of(key, dims, pieces, least, top_value):
    gain = 1.0
    for dim, shards_of in pieces:
        steps = jax.random.uniform(jax.random.fold_in(jax.random.fold_in(key, 6), dim), (shards_of,), jnp.float32, least / len(pieces), top_value / len(pieces))
        gain = gain * jnp.repeat(jnp.exp(steps), dims[dim] // shards_of).reshape((-1,) + (1,) * (len(dims) - 1 - dim))
    return gain


def scatter_about(stream_key, shape, width, most, cuts=(), held_as=jnp.bfloat16):
    result = jax.random.normal(stream_key, shape, jnp.float32) * width
    if len(cuts) > 0:
        result = steps_of(stream_key, shape, cuts, -0.22, 0.18) * result
    return jnp.clip(result, min=-most, max=most).astype(held_as)


def heavy_noise(stream_key, extent, spread, reach, cuts, heavy, kind=jnp.bfloat16):
    values = spread * jax.random.normal(stream_key, extent, jnp.float32)
    if cuts:
        values = values * steps_of(stream_key, extent, cuts, -0.22, 0.18)
    return jnp.clip(spiked(values, jax.random.fold_in(stream_key, 3), *heavy), -reach, reach).astype(kind)


def setup_inputs(seed: int = 0) -> dict:
    splits = jax.random.split(jax.random.key(seed), 4)
    amplitudes = heavy_noise(splits[0], (NIJ, CD), 1.0, 6.0, ((0, 16), (1, 32)), (1, 0, 32, 2.75), jnp.float32)
    integrals = scatter_about(splits[1], (AB, CD), CD ** -0.5, 0.01953125, ((0, 16), (1, 32)), jnp.float32)
    mirror_slot = draw_mirror_slot(jax.random.fold_in(splits[3], 71), 0)
    return {"amplitudes": amplitudes, "integrals": integrals, "mirror_slot": mirror_slot}


def reference(amplitudes, integrals, mirror_slot):
    ladder = lax.dot_general(integrals, amplitudes, (((1,), (1,)), ((), ())), precision=lax.Precision.HIGHEST, preferred_element_type=jnp.float32)
    row_width = NIJ // N_VC
    owners = jnp.arange(NIJ, dtype=jnp.int32) // row_width
    mirror_cols = ((owners + N_VC // 2) % N_VC) * row_width + mirror_slot.astype(jnp.int32)
    return ladder - jnp.take(ladder, mirror_cols, axis=1)
```

```python
import jax
import jax.numpy as jnp
from jax import lax
from jax.sharding import PartitionSpec as P

FIRST = (9, 0, 8, 1)
HIGH = lax.Precision.HIGH
HIGHEST = lax.Precision.HIGHEST


def move_z(value, step):
    return lax.ppermute(value, "vr", [(4 * z + y, 4 * ((z + step) % 4) + y) for z in range(4) for y in range(4)])


def move_y(value, step):
    return lax.ppermute(value, "vr", [(4 * z + y, 4 * z + (y + step) % 4) for z in range(4) for y in range(4)])


def move_x(value, step):
    return lax.ppermute(value, "vc", [(8 * x + r, 8 * ((x + step) % 4) + r) for x in range(4) for r in range(8)])


def move_low(value, step):
    pairs = [(8 * x + 2 * k + c, 8 * x + 2 * ((k + step) % 4) + c) for x in range(4) for k in range(4) for c in range(2)]
    return lax.ppermute(value, "vc", pairs)


def move_core(value):
    return lax.ppermute(value, "vc", [(c, c ^ 1) for c in range(32)])


def slots_of_my_block(mirror_slot):
    pairs = []
    for z in range(4):
        for y in range(4):
            block = FIRST[z] + 2 * y
            for i in range(16):
                pairs.append((32 * i + block, 32 * (4 * z + y) + i))
                pairs.append((32 * i + block + 16, 32 * (4 * z + y) + i + 16))
    return lax.ppermute(mirror_slot, ("vr", "vc"), pairs)


def all_y(value):
    return jnp.concatenate([value, move_y(value, 3), move_y(value, 2), move_y(value, 1)], 0)


def rolled(blocks, start):
    n = blocks.shape[0]
    return lax.dynamic_slice_in_dim(jnp.concatenate([blocks, blocks], 0), (n - start) % n, n, 0)


def local(amplitudes, integrals, mirror_slot):
    vr, vc = lax.axis_index("vr"), lax.axis_index("vc")
    z, y = vr // 4, vr % 4
    x, low, core = vc // 8, vc // 2 % 4, vc % 2
    iota = jnp.arange(32, dtype=jnp.int32)

    slots = slots_of_my_block(mirror_slot)
    up = lax.dynamic_slice_in_dim(amplitudes, 32 * (z // 2), 32, 0)
    down = lax.dynamic_slice_in_dim(amplitudes, 32 * (1 - z // 2), 32, 0)
    below, above = move_z(up, 1), move_z(down, 3)
    middle = (z == 1) | (z == 2)
    first, second = jnp.where(middle, below, above), jnp.where(middle, above, below)
    chosen = jnp.where(vc < 16, slots[:, None] == iota[None, :], slots[None, :] == iota[:, None])
    mine = first - jnp.dot(chosen.astype(jnp.float32), second, precision=HIGHEST)

    from_below, from_above = move_z(mine, 1), move_z(mine, 3)
    far = jnp.concatenate([move_z(from_below[:16], 1), move_z(from_above[16:], 3)], 0)

    def product(value):
        return lax.dot_general(value, integrals, (((1,), (1,)), ((), ())), precision=HIGH, preferred_element_type=jnp.float32)

    parts = [rolled(product(all_y(v)).reshape(4, 32, 320), y) for v in (mine, from_above, far, from_below)]
    parts = rolled(jnp.stack(parts), z)

    even, odd = jnp.stack([parts[1], parts[2]]), jnp.stack([parts[3], parts[0]])
    total = jnp.where(core == 0, even, odd) + move_core(jnp.where(core == 0, odd, even))
    odd_x = x % 2 == 1
    kept, given = jnp.where(odd_x, total[1], total[0]), jnp.where(odd_x, total[0], total[1])
    total = kept + move_x(kept, 2) + move_x(given, 1) + move_x(given, 3)
    at = [lax.dynamic_index_in_dim(total, (low + d) % 4, 0, False) for d in range(4)]
    total = at[0] + move_low(at[1], 1) + move_low(at[2], 2) + move_low(at[3], 3)

    slot = jnp.where(vc < 16, iota, mirror_slot)
    signed = jnp.where(slot[:, None] == iota[None, :], jnp.where(vc < 16, 1.0, -1.0), 0.0)
    return jnp.dot(signed, total, precision=HIGHEST).T


def solution(mesh):
    in_specs = (P("vr", "vc"), P("vr", "vc"), P("vc"))
    out_specs = P("vr", "vc")
    return jax.shard_map(local, mesh=mesh, in_specs=in_specs, out_specs=out_specs, check_vma=False)
```

```python
import jax
import jax.numpy as jnp
from jax import lax
from jax.sharding import PartitionSpec as P

FIRST = (0, 8, 1, 9)
HIGH = lax.Precision.HIGH
HIGHEST = lax.Precision.HIGHEST


def move_z(value, step):
    return lax.ppermute(value, "vr", [(4 * z + y, 4 * ((z + step) % 4) + y) for z in range(4) for y in range(4)])


def move_y(value, step):
    return lax.ppermute(value, "vr", [(4 * z + y, 4 * z + (y + step) % 4) for z in range(4) for y in range(4)])


def move_x(value, step):
    return lax.ppermute(value, "vc", [(8 * x + r, 8 * ((x + step) % 4) + r) for x in range(4) for r in range(8)])


def move_low(value, step):
    pairs = [(8 * x + 2 * k + c, 8 * x + 2 * ((k + step) % 4) + c) for x in range(4) for k in range(4) for c in range(2)]
    return lax.ppermute(value, "vc", pairs)


def move_core(value):
    return lax.ppermute(value, "vc", [(c, c ^ 1) for c in range(32)])


def slots_of_my_block(mirror_slot):
    pairs = []
    for z in range(4):
        for y in range(4):
            block = FIRST[z] + 2 * y
            for i in range(16):
                pairs.append((32 * i + block, 32 * (4 * z + y) + i))
                pairs.append((32 * i + block + 16, 32 * (4 * z + y) + i + 16))
    return lax.ppermute(mirror_slot, ("vr", "vc"), pairs)


SAME_CORE = [[8 * x + 2 * k + c for x in range(4) for k in range(4)] for c in range(2)]
SAME_PAIR = [[8 * x + 2 * k + c for x in (p, p + 1) for k in range(4)] for p in (0, 2) for c in range(2)]
SAME_Z = [[4 * z + y for y in range(4)] for z in range(4)]


SAME_Y = [[4 * z + y for z in range(4)] for y in range(4)]


def all_y(value):
    copies = jnp.broadcast_to(value[None], (4,) + value.shape)
    return lax.all_to_all(copies, "vr", 0, 0, axis_index_groups=SAME_Z)


def all_y_gather(value):
    return lax.all_gather(value, "vr", axis=0, axis_index_groups=SAME_Z)


def all_z(value):
    return lax.all_gather(value, "vr", axis=0, axis_index_groups=SAME_Y)


def local(amplitudes, integrals, mirror_slot):
    vr, vc = lax.axis_index("vr"), lax.axis_index("vc")
    z = vr // 4
    x, core = vc // 8, vc % 2
    iota = jnp.arange(32, dtype=jnp.int32)
    low_half = z < 2

    half = 32 * (z // 2)
    kept = lax.dynamic_slice_in_dim(amplitudes, half, 32, 0)
    other = move_z(lax.dynamic_slice_in_dim(amplitudes, 32 - half, 32, 0), 2)
    slots = slots_of_my_block(mirror_slot)
    chosen = jnp.where(vc < 16, slots[:, None] == iota[None, :], slots[None, :] == iota[:, None])
    first, second = jnp.where(low_half, kept, other), jnp.where(low_half, other, kept)
    mine = first - jnp.dot(chosen.astype(jnp.float32), second, precision=HIGHEST)

    def product(value):
        rows = value.shape[1]
        value = lax.dot_general(value.reshape(4 * rows, -1), integrals, (((1,), (1,)), ((), ())), precision=HIGH, preferred_element_type=jnp.float32)
        return value.reshape(4, rows, 320)

    def others(value):
        return jnp.concatenate([lax.dynamic_index_in_dim(value, (z + d) % 4, 0, False) for d in (1, 2, 3)], 0)

    own = all_y(mine)
    upper = all_z(mine[:16])
    lower, own = lax.optimization_barrier((mine[16:], own))
    upper = all_y(others(upper))
    lower = all_z(lower)
    lower, upper = lax.optimization_barrier((lower, upper))
    lower = all_y(others(lower))

    own, upper = lax.optimization_barrier((product(own), product(upper)))
    lower = product(lower)
    above, far, below = [jnp.concatenate([upper[:, 16 * d : 16 * d + 16], lower[:, 16 * d : 16 * d + 16]], 1) for d in range(3)]

    own_core = (z >= 2) == (core == 1)
    above_core = ((z == 1) | (z == 2)) == (core == 1)
    pick = lambda test, a, b: (jnp.where(test, a, b), jnp.where(test, b, a))
    kept, given = pick(own_core, own, far)
    kept2, given2 = pick(above_core, above, below)
    total = jnp.stack([kept, kept2]) + move_core(jnp.stack([given, given2]))
    total = jnp.where(z % 2 == 1, total[::-1], total)
    total = jnp.sum(lax.all_to_all(total.reshape(8, 32, 320), "vc", 0, 0, axis_index_groups=SAME_PAIR), 0)
    total = total + move_x(total, 2)

    slot = jnp.where(vc < 16, iota, mirror_slot)
    signed = jnp.where(slot[:, None] == iota[None, :], jnp.where(vc < 16, 1.0, -1.0), 0.0)
    return jnp.dot(signed, total, precision=HIGHEST).T


def solution(mesh):
    in_specs = (P("vr", "vc"), P("vr", "vc"), P("vc"))
    out_specs = P("vr", "vc")
    return jax.shard_map(local, mesh=mesh, in_specs=in_specs, out_specs=out_specs, check_vma=False)
```

```python
import jax
import jax.numpy as jnp
from jax import lax
from jax.sharding import PartitionSpec as P

FIRST = (0, 8, 1, 9)
HIGH = lax.Precision.HIGH
HIGHEST = lax.Precision.HIGHEST


def move_z(value, step):
    return lax.ppermute(value, "vr", [(4 * z + y, 4 * ((z + step) % 4) + y) for z in range(4) for y in range(4)])


def move_y(value, step):
    return lax.ppermute(value, "vr", [(4 * z + y, 4 * z + (y + step) % 4) for z in range(4) for y in range(4)])


def move_x(value, step):
    return lax.ppermute(value, "vc", [(8 * x + r, 8 * ((x + step) % 4) + r) for x in range(4) for r in range(8)])


def move_low(value, step):
    pairs = [(8 * x + 2 * k + c, 8 * x + 2 * ((k + step) % 4) + c) for x in range(4) for k in range(4) for c in range(2)]
    return lax.ppermute(value, "vc", pairs)


def move_core(value):
    return lax.ppermute(value, "vc", [(c, c ^ 1) for c in range(32)])


def slots_of_my_block(mirror_slot):
    pairs = []
    for z in range(4):
        for y in range(4):
            block = FIRST[z] + 2 * y
            for i in range(16):
                pairs.append((32 * i + block, 32 * (4 * z + y) + i))
                pairs.append((32 * i + block + 16, 32 * (4 * z + y) + i + 16))
    return lax.ppermute(mirror_slot, ("vr", "vc"), pairs)


SAME_CORE = [[8 * x + 2 * k + c for x in range(4) for k in range(4)] for c in range(2)]
SAME_PAIR = [[8 * x + 2 * k + c for x in (p, p + 1) for k in range(4)] for p in (0, 2) for c in range(2)]
SAME_Z = [[4 * z + y for y in range(4)] for z in range(4)]


SAME_Y = [[4 * z + y for z in range(4)] for y in range(4)]


def all_y(value):
    copies = jnp.broadcast_to(value[None], (4,) + value.shape)
    return lax.all_to_all(copies, "vr", 0, 0, axis_index_groups=SAME_Z)


def all_y_gather(value):
    return lax.all_gather(value, "vr", axis=0, axis_index_groups=SAME_Z)


def all_z(value):
    return lax.all_gather(value, "vr", axis=0, axis_index_groups=SAME_Y)


def local(amplitudes, integrals, mirror_slot):
    vr, vc = lax.axis_index("vr"), lax.axis_index("vc")
    z = vr // 4
    x, core = vc // 8, vc % 2
    iota = jnp.arange(32, dtype=jnp.int32)
    low_half = z < 2

    half = 32 * (z // 2)
    kept = lax.dynamic_slice_in_dim(amplitudes, half, 32, 0)
    other = move_z(lax.dynamic_slice_in_dim(amplitudes, 32 - half, 32, 0), 2)
    slots = slots_of_my_block(mirror_slot)
    chosen = jnp.where(vc < 16, slots[:, None] == iota[None, :], slots[None, :] == iota[:, None])
    first, second = jnp.where(low_half, kept, other), jnp.where(low_half, other, kept)
    mine = first - jnp.dot(chosen.astype(jnp.float32), second, precision=HIGHEST)

    def product(value):
        rows = value.shape[1]
        count = value.shape[0]
        value = lax.dot_general(value.reshape(count * rows, -1), integrals, (((1,), (1,)), ((), ())), precision=HIGH, preferred_element_type=jnp.float32)
        return value.reshape(count, rows, 320)

    def others(value):
        return jnp.concatenate([lax.dynamic_index_in_dim(value, (z + d) % 4, 0, False) for d in (1, 2, 3)], 0)

    own = all_y(mine)
    upper = all_z(mine[:16])
    lower, own = lax.optimization_barrier((mine[16:], own))
    upper = all_y(others(upper))
    lower = all_z(lower)
    lower, upper = lax.optimization_barrier((lower, upper))
    lower = others(lower)
    last_y, next_y = move_y(lower, 1), move_y(lower, 3)
    far_y = jnp.concatenate([move_y(last_y[:24], 1), move_y(next_y[24:], 3)], 0)

    own, upper = lax.optimization_barrier((product(own), product(upper)))
    lower = product(jnp.stack([lower, next_y, last_y]))
    far_y = product(far_y[None])
    lower = jnp.stack([lower[0], lower[1], far_y[0], lower[2]])
    lower = lax.dynamic_slice_in_dim(jnp.concatenate([lower, lower], 0), (4 - vr % 4) % 4, 4, 0)
    above, far, below = [jnp.concatenate([upper[:, 16 * d : 16 * d + 16], lower[:, 16 * d : 16 * d + 16]], 1) for d in range(3)]

    own_core = (z >= 2) == (core == 1)
    above_core = ((z == 1) | (z == 2)) == (core == 1)
    pick = lambda test, a, b: (jnp.where(test, a, b), jnp.where(test, b, a))
    kept, given = pick(own_core, own, far)
    kept2, given2 = pick(above_core, above, below)
    total = jnp.stack([kept, kept2]) + move_core(jnp.stack([given, given2]))
    total = jnp.where(z % 2 == 1, total[::-1], total)
    total = jnp.sum(lax.all_to_all(total.reshape(8, 32, 320), "vc", 0, 0, axis_index_groups=SAME_PAIR), 0)
    total = total + move_x(total, 2)

    slot = jnp.where(vc < 16, iota, mirror_slot)
    signed = jnp.where(slot[:, None] == iota[None, :], jnp.where(vc < 16, 1.0, -1.0), 0.0)
    return jnp.dot(signed, total, precision=HIGHEST).T


def solution(mesh):
    in_specs = (P("vr", "vc"), P("vr", "vc"), P("vc"))
    out_specs = P("vr", "vc")
    return jax.shard_map(local, mesh=mesh, in_specs=in_specs, out_specs=out_specs, check_vma=False)
```

```python
import jax
import jax.numpy as jnp
from jax import lax
from jax.sharding import PartitionSpec as P

FIRST = (0, 8, 1, 9)
CUT = 1664
HIGH = lax.Precision.HIGH
HIGHEST = lax.Precision.HIGHEST


def move_z(value, step):
    return lax.ppermute(value, "vr", [(4 * z + y, 4 * ((z + step) % 4) + y) for z in range(4) for y in range(4)])


def move_y(value, step):
    return lax.ppermute(value, "vr", [(4 * z + y, 4 * z + (y + step) % 4) for z in range(4) for y in range(4)])


def move_x(value, step):
    return lax.ppermute(value, "vc", [(8 * x + r, 8 * ((x + step) % 4) + r) for x in range(4) for r in range(8)])


def move_low(value, step):
    pairs = [(8 * x + 2 * k + c, 8 * x + 2 * ((k + step) % 4) + c) for x in range(4) for k in range(4) for c in range(2)]
    return lax.ppermute(value, "vc", pairs)


def move_core(value):
    return lax.ppermute(value, "vc", [(c, c ^ 1) for c in range(32)])


def slots_of_my_block(mirror_slot):
    pairs = []
    for z in range(4):
        for y in range(4):
            block = FIRST[z] + 2 * y
            for i in range(16):
                pairs.append((32 * i + block, 32 * (4 * z + y) + i))
                pairs.append((32 * i + block + 16, 32 * (4 * z + y) + i + 16))
    return lax.ppermute(mirror_slot, ("vr", "vc"), pairs)


SAME_CORE = [[8 * x + 2 * k + c for x in range(4) for k in range(4)] for c in range(2)]
SAME_PAIR = [[8 * x + 2 * k + c for x in (p, p + 1) for k in range(4)] for p in (0, 2) for c in range(2)]
SAME_Z = [[4 * z + y for y in range(4)] for z in range(4)]


SAME_Y = [[4 * z + y for z in range(4)] for y in range(4)]


def all_y(value):
    copies = jnp.broadcast_to(value[None], (4,) + value.shape)
    return lax.all_to_all(copies, "vr", 0, 0, axis_index_groups=SAME_Z)


def all_y_gather(value):
    return lax.all_gather(value, "vr", axis=0, axis_index_groups=SAME_Z)


def all_z(value):
    return lax.all_gather(value, "vr", axis=0, axis_index_groups=SAME_Y)


def local(amplitudes, integrals, mirror_slot):
    vr, vc = lax.axis_index("vr"), lax.axis_index("vc")
    z = vr // 4
    x, core = vc // 8, vc % 2
    iota = jnp.arange(32, dtype=jnp.int32)
    low_half = z < 2

    half = 32 * (z // 2)
    kept = lax.dynamic_slice_in_dim(amplitudes, half, 32, 0)
    other = move_z(lax.dynamic_slice_in_dim(amplitudes, 32 - half, 32, 0), 2)
    slots = slots_of_my_block(mirror_slot)
    chosen = jnp.where(vc < 16, slots[:, None] == iota[None, :], slots[None, :] == iota[:, None])
    first, second = jnp.where(low_half, kept, other), jnp.where(low_half, other, kept)
    mine = first - jnp.dot(chosen.astype(jnp.float32), second, precision=HIGHEST)

    def product(value, integrals):
        count, rows = value.shape[:2]
        value = lax.dot_general(value.reshape(count * rows, -1), integrals, (((1,), (1,)), ((), ())), precision=HIGH, preferred_element_type=jnp.float32)
        return value.reshape(count, rows, 320)

    def others(value):
        return jnp.concatenate([lax.dynamic_index_in_dim(value, (z + d) % 4, 0, False) for d in (1, 2, 3)], 0)

    own = all_y(mine)
    early = all_z(mine[:, :CUT])
    late, own = lax.optimization_barrier((mine[:, CUT:], own))
    early = all_y(others(early))
    late = all_z(late)
    late, early = lax.optimization_barrier((late, early))
    late = others(late)
    last_y, next_y = move_y(late, 1), move_y(late, 3)
    far_y = jnp.concatenate([move_y(last_y[:48], 1), move_y(next_y[48:], 3)], 0)

    own, early = lax.optimization_barrier((product(own, integrals), product(early, integrals[:, :CUT])))
    late = product(jnp.stack([late, next_y, last_y]), integrals[:, CUT:])
    far_y = product(far_y[None], integrals[:, CUT:])
    late = jnp.stack([late[0], late[1], far_y[0], late[2]])
    late = lax.dynamic_slice_in_dim(jnp.concatenate([late, late], 0), (4 - vr % 4) % 4, 4, 0)
    total = early + late
    above, far, below = total[:, :32], total[:, 32:64], total[:, 64:]

    own_core = (z >= 2) == (core == 1)
    above_core = ((z == 1) | (z == 2)) == (core == 1)
    pick = lambda test, a, b: (jnp.where(test, a, b), jnp.where(test, b, a))
    kept, given = pick(own_core, own, far)
    kept2, given2 = pick(above_core, above, below)
    total = jnp.stack([kept, kept2]) + move_core(jnp.stack([given, given2]))
    total = jnp.where(z % 2 == 1, total[::-1], total)
    total = jnp.sum(lax.all_to_all(total.reshape(8, 32, 320), "vc", 0, 0, axis_index_groups=SAME_PAIR), 0)
    total = total + move_x(total, 2)

    slot = jnp.where(vc < 16, iota, mirror_slot)
    signed = jnp.where(slot[:, None] == iota[None, :], jnp.where(vc < 16, 1.0, -1.0), 0.0)
    return jnp.dot(signed, total, precision=HIGHEST).T


def solution(mesh):
    in_specs = (P("vr", "vc"), P("vr", "vc"), P("vc"))
    out_specs = P("vr", "vc")
    return jax.shard_map(local, mesh=mesh, in_specs=in_specs, out_specs=out_specs, check_vma=False)
```
